256 devices in a mesh: seq: 128 (over y_lo, z, x, core), ch: 2 (over y_hi).
Axes of the slice: x: 4, y: 4 (y_hi: 2, y_lo: 2; y = y_hi * 2 + y_lo), z: 8, core: 2. Of those that a mesh axis runs over, the one named last changes fastest.
Arguments:
- inputs: bfloat16 [2, 384, 262144], P(None, 'ch', 'seq'), may hold values from -6 to 6
- convolution_weight: bfloat16 [3, 384, 384], P(None, 'ch'), may hold values from -0.1875 to 0.1875
- conv_bias: float32 [384], P('ch'), may hold values from -3 to 3
- mix_weight: bfloat16 [384, 384], P('ch'), may hold values from -0.3125 to 0.3125
- cotangent: bfloat16 [2, 384, 262144], P(None, 'ch', 'seq'), may hold values from -6 to 6
Outputs:
- outputs: bfloat16 [2, 384, 262144], P(None, 'ch', 'seq')
- input_grad: bfloat16 [2, 384, 262144], P(None, 'ch', 'seq')
- conv_weight_grad: float32 [3, 384, 384], P(None, 'ch')
- conv_bias_grad: float32 [384], P('ch')
- mix_weight_grad: float32 [384, 384], P('ch')
The draws below stay inside these ranges and needn't reach their ends.
All inputs are finite; a program needn't handle non-finite values.
Results may differ from the reference program's by a relative error of at most 0.007.
Values may be sent and summed in bfloat16 or wider, within the bound.
No kernel may reach another device: no remote copies, remote signals or barrier semaphores. Data moves between devices by JAX's collectives and lax.ppermute only.
A program may use at most 128 MiB of HBM per device.

```python
import math
import jax
import jax.numpy as jnp
from jax import lax

C = 384
BATCH = 2
LENGTH = 262144
DILATION_STEP = 4096


def block_scale(stream_key, shape, split, low, high):
    factor_of, own = 1.0, jax.random.fold_in(stream_key, 6)
    for dim, parts in split:
        steps = jnp.exp(jax.random.uniform(jax.random.fold_in(own, dim), (parts,), jnp.float32, low / len(split), high / len(split)))
        factor_of = factor_of * jnp.repeat(steps, shape[dim] // parts).reshape([-1 if axis == dim else 1 for axis in range(len(shape))])
    return factor_of


def scatter_about(stream_key, shape, width, limit, cuts=(), kind=jnp.bfloat16):
    entries = width * jax.random.normal(stream_key, shape, jnp.float32)
    if cuts:
        entries = entries * block_scale(stream_key, shape, cuts, -0.22, 0.18)
    return jnp.clip(entries, -limit, limit).astype(kind)


def setup_inputs(seed: int = 0) -> dict:
    streams_of = jax.random.split(jax.random.key(seed), 6)
    return {
        "inputs": scatter_about(streams_of[0], (BATCH, C, LENGTH), 1.0, 6.0, ((1, 2), (2, 128))),
        "convolution_weight": scatter_about(streams_of[1], (3, C, C), (3 * C) ** -0.5, 0.1875, ((1, 2),)),
        "conv_bias": scatter_about(streams_of[2], (C,), 0.5, 3.0, ((0, 2),), jnp.float32),
        "mix_weight": scatter_about(streams_of[3], (C, C), C ** -0.5, 0.3125, ((0, 2),)),
        "cotangent": scatter_about(streams_of[4], (BATCH, C, LENGTH), 1.0, 6.0, ((1, 2), (2, 128))),
    }


def shift_toward_end(receptive_field, span):
    blank = jnp.zeros((receptive_field.shape[0], span), receptive_field.dtype)
    return jnp.concatenate([blank, receptive_field[:, :-span]], axis=1)

def shift_toward_start(receptive_field, span):
    blank = jnp.zeros((receptive_field.shape[0], span), receptive_field.dtype)
    return jnp.concatenate([receptive_field[:, span:], blank], axis=1)

def gelu_grad(pre, upstream):
    return jax.vjp(jax.nn.gelu, pre)[1](upstream)[0]

def reference(inputs, convolution_weight, conv_bias, mix_weight, cotangent):
    out_list = []
    grad_list = []
    weight_acc = jnp.zeros((3, C, C), jnp.float32)
    bias_acc = jnp.zeros((C,), jnp.float32)
    mix_acc = jnp.zeros((C, C), jnp.float32)
    for member in range(BATCH):
        receptive_field = inputs[member]
        trailing_tap_slice = shift_toward_end(receptive_field, DILATION_STEP)
        forward_tap_slice = shift_toward_start(receptive_field, DILATION_STEP)
        pre = jnp.dot(convolution_weight[0], trailing_tap_slice, preferred_element_type=jnp.float32)
        pre = pre + jnp.dot(convolution_weight[1], receptive_field, preferred_element_type=jnp.float32)
        pre = pre + jnp.dot(convolution_weight[2], forward_tap_slice, preferred_element_type=jnp.float32)
        pre = pre + conv_bias.astype(jnp.float32)[:, None]
        activated = jax.nn.gelu(pre).astype(jnp.bfloat16)
        result = receptive_field.astype(jnp.float32) + jnp.dot(mix_weight, activated, preferred_element_type=jnp.float32)
        out_list.append(result.astype(jnp.bfloat16))
        upstream = cotangent[member]
        mix_acc = mix_acc + jnp.dot(upstream, activated.T, preferred_element_type=jnp.float32)
        grad_act = jnp.dot(mix_weight.T, upstream, preferred_element_type=jnp.float32)
        preactivation_gradient = gelu_grad(pre, grad_act).astype(jnp.bfloat16)
        weight_acc = weight_acc + jnp.stack([jnp.dot(preactivation_gradient, trailing_tap_slice.T, preferred_element_type=jnp.float32), jnp.dot(preactivation_gradient, receptive_field.T, preferred_element_type=jnp.float32), jnp.dot(preactivation_gradient, forward_tap_slice.T, preferred_element_type=jnp.float32)])
        bias_acc = bias_acc + lax.optimization_barrier(jnp.sum(preactivation_gradient.astype(jnp.float32), axis=1))
        backward_result = jnp.dot(convolution_weight[0].T, shift_toward_start(preactivation_gradient, DILATION_STEP), preferred_element_type=jnp.float32)
        backward_result = backward_result + jnp.dot(convolution_weight[1].T, preactivation_gradient, preferred_element_type=jnp.float32)
        backward_result = backward_result + jnp.dot(convolution_weight[2].T, shift_toward_end(preactivation_gradient, DILATION_STEP), preferred_element_type=jnp.float32)
        grad_list.append((upstream.astype(jnp.float32) + backward_result).astype(jnp.bfloat16))
    factor = 1.0 / math.sqrt(BATCH * LENGTH)
    return (jnp.stack(out_list), jnp.stack(grad_list), weight_acc * factor, bias_acc * factor, mix_acc * factor)
```

```python
import math

import jax
import jax.numpy as jnp
from jax import lax
from jax.experimental import pallas as pl
from jax.experimental.pallas import tpu as pltpu
from jax.sharding import PartitionSpec as P

BF16, F32 = jnp.bfloat16, jnp.float32
AXES = ("seq", "ch")
CHUNKS = 2
SIZE = 1024 // CHUNKS
TILE = 512
ROOT = math.sqrt(2.0 / math.pi)
CUBE = 0.044715


def route(target):
    pairs = []
    for s in range(128):
        for h in range(2):
            to = target(s, h)
            pairs.append((2 * s + h, 2 * to[0] + to[1]))
    return pairs


def send(block, target):
    return lax.ppermute(block, AXES, route(target))


def other_ch(s, h):
    return s, 1 - h


def other_core(s, h):
    return s ^ 1, h


def along_x(step):
    return lambda s, h: ((s & ~6) | ((((s >> 1) + step) & 3) << 1), h)


def flip(bits):
    return lambda s, h: (s ^ bits, h)


def chips_on(step):
    return lambda s, h: ((s & 64) | ((s + 2 * step) & 63), h)


def column_groups():
    return [[2 * (64 * (y & 1) + place) + (y >> 1) for y in range(4)] for place in range(64)]


def exchange(block):
    return lax.all_to_all(block, AXES, 0, 0, axis_index_groups=column_groups())


def dot(a, b, dims=((1,), (0,))):
    return lax.dot_general(a, b, (dims, ((), ())), preferred_element_type=F32)


def params(megabytes=28):
    return pltpu.CompilerParams(vmem_limit_bytes=megabytes * 2**20)


def copy_kernel(source, target):
    target[...] = source[...]


def pack(array, k):
    block = (1, 192, SIZE)
    return pl.pallas_call(
        copy_kernel,
        grid=(4,),
        in_specs=[pl.BlockSpec(block, lambda d: (d // 2, 0, (d % 2) * CHUNKS + k))],
        out_specs=pl.BlockSpec(block, lambda d: (d, 0, 0)),
        out_shape=jax.ShapeDtypeStruct((4, 192, SIZE), BF16),
        compiler_params=params(),
        cost_estimate=pl.CostEstimate(flops=0, bytes_accessed=16 * 192 * SIZE, transcendentals=0),
    )(array)


def unpack_kernel(*refs):
    for k, source in enumerate(refs[:-1]):
        width = source.shape[2]
        refs[-1][:, :, k * width : (k + 1) * width] = source[...]


def unpack(pieces):
    width = pieces[0].shape[2]
    return pl.pallas_call(
        unpack_kernel,
        grid=(4,),
        in_specs=[pl.BlockSpec((1, 192, width), lambda d: (d, 0, 0))] * len(pieces),
        out_specs=pl.BlockSpec((1, 192, 1024), lambda d: (d // 2, 0, d % 2)),
        out_shape=jax.ShapeDtypeStruct((2, 192, 2048), BF16),
        compiler_params=params(),
        cost_estimate=pl.CostEstimate(flops=0, bytes_accessed=16 * 192 * 1024, transcendentals=0),
    )(*pieces)


def weights_kernel(taps, mix, bias, out):
    for k in range(3):
        out[:, 384 * k : 384 * (k + 1)] = taps[k]
    out[:, 1152:1536] = mix[...]
    value = jnp.broadcast_to(bias[...], (192, 128))
    high = value.astype(BF16).astype(F32)
    middle = (value - high).astype(BF16).astype(F32)
    low = value - high - middle
    lane = lax.broadcasted_iota(jnp.int32, (192, 128), 1)
    split = jnp.where(lane == 0, high, jnp.where(lane == 1, middle, jnp.where(lane == 2, low, 0.0)))
    out[:, 1536:1664] = split.astype(BF16)


def pack_weights(taps, mix, bias):
    return pl.pallas_call(
        weights_kernel,
        out_shape=jax.ShapeDtypeStruct((192, 1664), BF16),
        compiler_params=params(),
    )(taps, mix, bias.reshape(192, 1))


def rows(ref):
    return ref[...].reshape(384, TILE)


def masked(ref, keep):
    return jnp.where(keep == 1, rows(ref), jnp.zeros((384, TILE), BF16))


def middle_kernel(edge, behind, here, ahead, cot, weights, *refs):
    so_far, (out, grad_pre, sums) = refs[:-3], refs[-3:]
    group = pl.program_id(0)

    @pl.when((group == 0) & (pl.program_id(1) == 0))
    def _():
        sums[...] = so_far[0][...] if so_far else jnp.zeros((384, 1664), F32)

    center = rows(here)
    field = jnp.concatenate(
        [masked(behind, edge[2 + group]), center, masked(ahead, edge[6 + group])], axis=0
    )
    bias = weights[:, 1536:1664].astype(F32)
    bias = bias[:, 0:1] + bias[:, 1:2] + bias[:, 2:3]
    pre = dot(weights[:, 0:1152], field) + bias
    square = pre * pre
    bent = jnp.tanh(ROOT * pre * (1.0 + CUBE * square))
    half = 0.5 * (1.0 + bent)
    act = (pre * half).astype(BF16)
    slope = half + 0.5 * pre * (1.0 - bent * bent) * (ROOT * (1.0 + 3.0 * CUBE * square))
    mix = weights[:, 1152:1536]
    out[...] = (center.astype(F32) + dot(mix, act)).astype(BF16).reshape(out.shape)
    upstream = rows(cot)
    grad = (dot(mix, upstream, ((0,), (0,))) * slope).astype(BF16)
    grad_pre[...] = grad.reshape(grad_pre.shape)
    last = ((1,), (1,))
    sums[:, 0:1152] += dot(grad, field, last)
    sums[:, 1152:1536] += dot(upstream, act, last)
    sums[:, 1536:1664] += jnp.broadcast_to(
        jnp.sum(grad.astype(F32), axis=1, keepdims=True), (384, 128)
    )


def tile_specs():
    block = (2, 1, 192, TILE)
    plain = pl.BlockSpec(block, lambda g, i, edge: (0, g, 0, i))
    behind = pl.BlockSpec(block, lambda g, i, edge: (0, edge[g], 0, i))
    ahead = pl.BlockSpec(block, lambda g, i, edge: (0, edge[4 + g], 0, i))
    return plain, behind, ahead


def whole(array):
    return pl.BlockSpec(array.shape, lambda g, i, edge: (0,) * array.ndim)


def middle(edge, behind, here, ahead, cot, weights, *so_far):
    plain, before, after = tile_specs()
    sums = jax.ShapeDtypeStruct((384, 1664), F32)
    field = jax.ShapeDtypeStruct((2, 2, 192, SIZE), BF16)
    return pl.pallas_call(
        middle_kernel,
        grid_spec=pltpu.PrefetchScalarGridSpec(
            num_scalar_prefetch=1,
            grid=(2, SIZE // TILE),
            in_specs=[before, plain, after, plain, whole(weights)] + [whole(a) for a in so_far],
            out_specs=[plain, plain, whole(sums)],
        ),
        out_shape=[field, field, sums],
        compiler_params=params(),
        cost_estimate=pl.CostEstimate(
            flops=36 * 384 * 384 * SIZE, bytes_accessed=24 * 384 * SIZE, transcendentals=768 * SIZE
        ),
    )(edge, behind, here, ahead, cot, weights, *so_far)


def back_kernel(edge, behind, here, ahead, cot, weights, out, taps):
    group = pl.program_id(0)

    @pl.when((group == 0) & (pl.program_id(1) == 0))
    def _():
        for k in range(3):
            tap = weights[:, 384 * (2 - k) : 384 * (3 - k)]
            taps[:, 384 * k : 384 * (k + 1)] = tap.T

    field = jnp.concatenate(
        [masked(behind, edge[2 + group]), rows(here), masked(ahead, edge[6 + group])], axis=0
    )
    result = (rows(cot).astype(F32) + dot(taps[...], field)).astype(BF16)
    out[...] = result.reshape(out.shape)


def back(edge, behind, here, ahead, cot, weights):
    plain, before, after = tile_specs()
    return pl.pallas_call(
        back_kernel,
        grid_spec=pltpu.PrefetchScalarGridSpec(
            num_scalar_prefetch=1,
            grid=(2, SIZE // TILE),
            in_specs=[before, plain, after, plain, whole(weights)],
            out_specs=plain,
            scratch_shapes=[pltpu.VMEM((384, 1152), BF16)],
        ),
        out_shape=jax.ShapeDtypeStruct((2, 2, 192, SIZE), BF16),
        compiler_params=params(),
        cost_estimate=pl.CostEstimate(
            flops=12 * 384 * 384 * SIZE, bytes_accessed=20 * 384 * SIZE, transcendentals=0
        ),
    )(edge, behind, here, ahead, cot, weights)


def pick(array, index, axis):
    return lax.dynamic_index_in_dim(array, index, axis, keepdims=False)


def choose(choices, index):
    found = choices[0]
    for k in range(1, len(choices)):
        found = jnp.where(index == k, choices[k], found)
    return found


def sum_over_devices(sums, factor):
    place, half = lax.axis_index("seq"), lax.axis_index("ch")
    core, x = place & 1, (place >> 1) & 3
    parts = sums.reshape(2, 2, 4, 24, 1664)
    both = pick(parts, core, 1) + send(pick(parts, 1 - core, 1), other_core)
    mine = pick(both, half, 0) + send(pick(both, 1 - half, 0).astype(BF16), other_ch).astype(F32)
    total = pick(mine, x, 0)
    for step in (1, 2, 3):
        part = pick(mine, (x + step) & 3, 0).astype(BF16)
        total = total + send(part, along_x(step)).astype(F32)
    for a, b in ((64, 8), (16, 32)):
        own = total.astype(BF16)
        first, second, third = (send(own, flip(m)).astype(F32) for m in (a, b, a ^ b))
        total = (own.astype(F32) + first) + (second + third)
    total = (total * factor).astype(BF16)
    found = [total] + [send(total, along_x(step)) for step in (1, 2, 3)]
    gathered = jnp.stack([choose(found, (x - to) & 3) for to in range(4)])
    across = send(gathered, other_core)
    first = jnp.where(core == 0, gathered, across)
    second = jnp.where(core == 0, across, gathered)
    return jnp.concatenate([first, second]).reshape(192, 1664).astype(F32)


def edges(chip):
    first, final = (chip == 0).astype(jnp.int32), (chip == 31).astype(jnp.int32)
    one, zero = jnp.int32(1), jnp.int32(0)
    return jnp.stack([zero, 1 - first, 1 - first, one, final, one, one, 1 - final])


def per_device(inputs, convolution_weight, conv_bias, mix_weight, cotangent):
    factor = 1.0 / math.sqrt(inputs.shape[0] * inputs.shape[2] * lax.axis_size("seq"))
    edge = edges((lax.axis_index("seq") >> 1) & 31)
    field = (2, 2, 192, SIZE)
    here = [exchange(pack(inputs, k)).reshape(field) for k in range(CHUNKS)]
    weights = pack_weights(convolution_weight, mix_weight, conv_bias)
    weights = lax.all_gather(weights, "ch", axis=0, tiled=True)
    cot = [exchange(pack(cotangent, k)).reshape(field) for k in range(CHUNKS)]
    sides = [(send(a, chips_on(1)), send(a, chips_on(-1))) for a in here]
    sums, outs, grads, grad_sides = (), [], [], []
    for k in range(CHUNKS):
        out, grad, *sums = middle(edge, sides[k][0], here[k], sides[k][1], cot[k], weights, *sums)
        outs.append(out)
        grads.append(grad)
        grad_sides.append((send(grad, chips_on(1)), send(grad, chips_on(-1))))

    def spread(pieces):
        return unpack([exchange(p.reshape(4, 192, p.shape[3])) for p in pieces])

    outputs = spread(outs)
    input_grad = spread(
        [
            back(edge, grad_sides[k][0], grads[k], grad_sides[k][1], cot[k], weights)
            for k in range(CHUNKS)
        ]
    )
    found = sum_over_devices(sums[0], factor)
    weight_grad = jnp.stack([found[:, 0:384], found[:, 384:768], found[:, 768:1152]])
    return outputs, input_grad, weight_grad, found[:, 1536], found[:, 1152:1536]


def solution(mesh):
    in_specs = (
        P(None, "ch", "seq"),
        P(None, "ch", None),
        P("ch"),
        P("ch", None),
        P(None, "ch", "seq"),
    )
    out_specs = (
        P(None, "ch", "seq"),
        P(None, "ch", "seq"),
        P(None, "ch", None),
        P("ch"),
        P("ch", None),
    )
    return jax.shard_map(
        per_device, mesh=mesh, in_specs=in_specs, out_specs=out_specs, check_vma=False
    )
```

```python
import math

import jax
import jax.numpy as jnp
from jax import lax
from jax.experimental import pallas as pl
from jax.experimental.pallas import tpu as pltpu
from jax.sharding import PartitionSpec as P

BF16, F32 = jnp.bfloat16, jnp.float32
AXES = ("seq", "ch")
CHUNKS = 1
SIZE = 1024 // CHUNKS
TILE = 512
ROOT = math.sqrt(2.0 / math.pi)
CUBE = 0.044715


def route(target):
    pairs = []
    for s in range(128):
        for h in range(2):
            to = target(s, h)
            pairs.append((2 * s + h, 2 * to[0] + to[1]))
    return pairs


def send(block, target):
    return lax.ppermute(block, AXES, route(target))


def other_ch(s, h):
    return s, 1 - h


def other_core(s, h):
    return s ^ 1, h


def flip(bits):
    return lambda s, h: (s ^ bits, h)


def chips_on(step):
    return lambda s, h: ((s & 64) | ((s + 2 * step) & 63), h)


def column_groups():
    return [[2 * (64 * (y & 1) + place) + (y >> 1) for y in range(4)] for place in range(64)]


def exchange(block):
    return lax.all_to_all(block, AXES, 0, 0, axis_index_groups=column_groups())


def dot(a, b, dims=((1,), (0,))):
    return lax.dot_general(a, b, (dims, ((), ())), preferred_element_type=F32)


def params(megabytes=28):
    return pltpu.CompilerParams(vmem_limit_bytes=megabytes * 2**20)


def copy_kernel(source, *refs):
    refs[-1][...] = source[...]


def pack(array, k, *after):
    block = (1, 192, SIZE)
    return pl.pallas_call(
        copy_kernel,
        grid=(4,),
        in_specs=[pl.BlockSpec(block, lambda d: (d // 2, 0, (d % 2) * CHUNKS + k))]
        + [pl.BlockSpec(memory_space=pl.ANY)] * len(after),
        out_specs=pl.BlockSpec(block, lambda d: (d, 0, 0)),
        out_shape=jax.ShapeDtypeStruct((4, 192, SIZE), BF16),
        compiler_params=params(),
        cost_estimate=pl.CostEstimate(flops=0, bytes_accessed=16 * 192 * SIZE, transcendentals=0),
    )(array, *after)


def split_kernel(place, *refs):
    for source, target in zip(refs[:4], refs[4:]):
        target[...] = source[0]


def split(array, place, k):
    def source(other_half, other_low):
        def index(i, place):
            half, low = place[0] ^ other_half, place[1] ^ other_low
            return half, 0, low * CHUNKS + k

        return pl.BlockSpec((1, 192, SIZE), index)

    plain = pl.BlockSpec((192, SIZE), lambda i, place: (0, 0))
    return pl.pallas_call(
        split_kernel,
        grid_spec=pltpu.PrefetchScalarGridSpec(
            num_scalar_prefetch=1,
            grid=(1,),
            in_specs=[source(0, 0), source(0, 1), source(1, 0), source(1, 1)],
            out_specs=[plain] * 4,
        ),
        out_shape=[jax.ShapeDtypeStruct((192, SIZE), BF16)] * 4,
        compiler_params=params(),
    )(place, array, array, array, array)


def join_kernel(place, own, low, half, both, out):
    for source, a, b in ((own, 0, 0), (low, 0, 1), (half, 1, 0), (both, 1, 1)):
        out[pl.ds(place[0] ^ a, 1), pl.ds(place[1] ^ b, 1)] = source[...][None, None]


def join(place, *parts):
    vmem = pl.BlockSpec(memory_space=pltpu.VMEM)
    return pl.pallas_call(
        join_kernel,
        in_specs=[pl.BlockSpec(memory_space=pltpu.SMEM)] + [vmem] * 4,
        out_specs=vmem,
        out_shape=jax.ShapeDtypeStruct((2, 2, 192, SIZE), BF16),
        compiler_params=params(),
    )(place, *parts)


def other_low(s, h):
    return s ^ 64, h


def other_both(s, h):
    return s ^ 64, 1 - h


def gather_column(array, place, k):
    own, low, half, both = split(array, place, k)
    return join(place, own, send(low, other_low), send(half, other_ch), send(both, other_both))


def unpack_kernel(source, target):
    target[0, :, 0:1024] = source[0]
    target[0, :, 1024:2048] = source[1]


def unpack(pieces):
    return pl.pallas_call(
        unpack_kernel,
        grid=(2,),
        in_specs=[pl.BlockSpec((2, 192, 1024), lambda d: (d, 0, 0))],
        out_specs=pl.BlockSpec((1, 192, 2048), lambda d: (d, 0, 0)),
        out_shape=jax.ShapeDtypeStruct((2, 192, 2048), BF16),
        compiler_params=params(),
        cost_estimate=pl.CostEstimate(flops=0, bytes_accessed=16 * 192 * 1024, transcendentals=0),
    )(pieces[0])


def weights_kernel(taps, mix, bias, *refs):
    out = refs[-1]
    for k in range(3):
        out[:, 384 * k : 384 * (k + 1)] = taps[k]
    out[:, 1152:1536] = mix[...]
    value = jnp.broadcast_to(bias[...], (192, 128))
    high = value.astype(BF16).astype(F32)
    middle = (value - high).astype(BF16).astype(F32)
    low = value - high - middle
    lane = lax.broadcasted_iota(jnp.int32, (192, 128), 1)
    split = jnp.where(lane == 0, high, jnp.where(lane == 1, middle, jnp.where(lane == 2, low, 0.0)))
    out[:, 1536:1664] = split.astype(BF16)


def pack_weights(taps, mix, bias, *after):
    return pl.pallas_call(
        weights_kernel,
        in_specs=[pl.BlockSpec(memory_space=pltpu.VMEM)] * 3
        + [pl.BlockSpec(memory_space=pl.ANY)] * len(after),
        out_shape=jax.ShapeDtypeStruct((192, 1664), BF16),
        compiler_params=params(),
    )(taps, mix, bias.reshape(192, 1), *after)


def assemble_kernel(place, own, straight, crossed, out):
    half, core = place[0], place[1]
    out[pl.ds(pl.multiple_of(192 * half, 192), 192), :] = own[...]
    base = 192 * (1 - half)
    out[pl.ds(pl.multiple_of(base + 96 * core, 96), 96), :] = straight[...]
    out[pl.ds(pl.multiple_of(base + 96 * (1 - core), 96), 96), :] = crossed[...]


def gather_weights(own, half, core):
    straight = send(pick(own.reshape(2, 96, 1664), core, 0), other_ch)
    crossed = send(straight, other_core)
    return pl.pallas_call(
        assemble_kernel,
        in_specs=[pl.BlockSpec(memory_space=pltpu.SMEM)]
        + [pl.BlockSpec(memory_space=pltpu.VMEM)] * 3,
        out_shape=jax.ShapeDtypeStruct((384, 1664), BF16),
        compiler_params=params(),
    )(jnp.stack([half, core]).astype(jnp.int32), own, straight, crossed)


def rows(ref):
    return ref[...].reshape(384, TILE)


def masked(ref, keep):
    return jnp.where(keep == 1, rows(ref), jnp.zeros((384, TILE), BF16))


def middle_kernel(edge, behind, here, ahead, cot, weights, *refs):
    act_out, grad_pre, own, theirs, sums = refs
    group = pl.program_id(0)

    @pl.when((group == 0) & (pl.program_id(1) == 0))
    def _():
        sums[...] = jnp.zeros((384, 1664), F32)

    center = rows(here)
    field = jnp.concatenate(
        [masked(behind, edge[2 + group]), center, masked(ahead, edge[6 + group])], axis=0
    )
    bias = weights[:, 1536:1664].astype(F32)
    bias = bias[:, 0:1] + bias[:, 1:2] + bias[:, 2:3]
    pre = dot(weights[:, 0:1152], field) + bias
    square = pre * pre
    bent = jnp.tanh(ROOT * pre * (1.0 + CUBE * square))
    half = 0.5 * (1.0 + bent)
    act = (pre * half).astype(BF16)
    slope = half + 0.5 * pre * (1.0 - bent * bent) * (ROOT * (1.0 + 3.0 * CUBE * square))
    mix = weights[:, 1152:1536]
    act_out[...] = act.reshape(act_out.shape)
    upstream = rows(cot)
    grad = (dot(mix, upstream, ((0,), (0,))) * slope).astype(BF16)
    grad_pre[...] = grad.reshape(grad_pre.shape)
    last = ((1,), (1,))
    sums[:, 0:1152] += dot(grad, field, last)
    sums[:, 1152:1536] += dot(upstream, act, last)
    sums[:, 1536:1664] += jnp.broadcast_to(
        jnp.sum(grad.astype(F32), axis=1, keepdims=True), (384, 128)
    )

    @pl.when((group == 1) & (pl.program_id(1) == pl.num_programs(1) - 1))
    def _():
        core = edge[8]
        for h in range(2):
            own[h] = sums[pl.ds(pl.multiple_of(192 * h + 96 * core, 96), 96), :]
            theirs[h] = sums[pl.ds(pl.multiple_of(192 * h + 96 * (1 - core), 96), 96), :]


def tile_specs():
    block = (2, 1, 192, TILE)
    plain = pl.BlockSpec(block, lambda g, i, edge: (0, g, 0, i))
    behind = pl.BlockSpec(block, lambda g, i, edge: (0, edge[g], 0, i))
    ahead = pl.BlockSpec(block, lambda g, i, edge: (0, edge[4 + g], 0, i))
    return plain, behind, ahead


def whole(array):
    return pl.BlockSpec(array.shape, lambda g, i, edge: (0,) * array.ndim)


def middle(edge, behind, here, ahead, cot, weights):
    plain, before, after = tile_specs()
    sums = jax.ShapeDtypeStruct((2, 96, 1664), F32)
    field = jax.ShapeDtypeStruct((2, 2, 192, SIZE), BF16)
    return pl.pallas_call(
        middle_kernel,
        grid_spec=pltpu.PrefetchScalarGridSpec(
            num_scalar_prefetch=1,
            grid=(2, SIZE // TILE),
            in_specs=[before, plain, after, plain, whole(weights)],
            out_specs=[plain, plain, whole(sums), whole(sums)],
            scratch_shapes=[pltpu.VMEM((384, 1664), F32)],
        ),
        out_shape=[field, field, sums, sums],
        compiler_params=params(),
        cost_estimate=pl.CostEstimate(
            flops=36 * 384 * 384 * SIZE, bytes_accessed=24 * 384 * SIZE, transcendentals=768 * SIZE
        ),
    )(edge, behind, here, ahead, cot, weights)


def mix_kernel(edge, here, act, weights, *refs):
    out = refs[-1]
    result = rows(here).astype(F32) + dot(weights[:, 1152:1536], rows(act))
    out[...] = result.astype(BF16).reshape(out.shape)


def mixed(edge, here, act, weights, *after):
    plain, _, _ = tile_specs()
    return pl.pallas_call(
        mix_kernel,
        grid_spec=pltpu.PrefetchScalarGridSpec(
            num_scalar_prefetch=1,
            grid=(2, SIZE // TILE),
            in_specs=[plain, plain, whole(weights)]
            + [pl.BlockSpec(memory_space=pl.ANY)] * len(after),
            out_specs=plain,
        ),
        out_shape=jax.ShapeDtypeStruct((2, 2, 192, SIZE), BF16),
        compiler_params=params(),
        cost_estimate=pl.CostEstimate(
            flops=4 * 384 * 384 * SIZE, bytes_accessed=12 * 384 * SIZE, transcendentals=0
        ),
    )(edge, here, act, weights, *after)


def back_kernel(edge, behind, here, ahead, cot, weights, *refs):
    out, taps = refs[-2:]
    group = pl.program_id(0)

    @pl.when((group == 0) & (pl.program_id(1) == 0))
    def _():
        for k in range(3):
            tap = weights[:, 384 * (2 - k) : 384 * (3 - k)]
            taps[:, 384 * k : 384 * (k + 1)] = tap.T

    field = jnp.concatenate(
        [masked(behind, edge[2 + group]), rows(here), masked(ahead, edge[6 + group])], axis=0
    )
    result = (rows(cot).astype(F32) + dot(taps[...], field)).astype(BF16)
    out[...] = result.reshape(out.shape)


def back(edge, behind, here, ahead, cot, weights, *after):
    plain, before, beyond = tile_specs()
    return pl.pallas_call(
        back_kernel,
        grid_spec=pltpu.PrefetchScalarGridSpec(
            num_scalar_prefetch=1,
            grid=(2, SIZE // TILE),
            in_specs=[before, plain, beyond, plain, whole(weights)]
            + [pl.BlockSpec(memory_space=pl.ANY)] * len(after),
            out_specs=plain,
            scratch_shapes=[pltpu.VMEM((384, 1152), BF16)],
        ),
        out_shape=jax.ShapeDtypeStruct((2, 2, 192, SIZE), BF16),
        compiler_params=params(),
        cost_estimate=pl.CostEstimate(
            flops=12 * 384 * 384 * SIZE, bytes_accessed=20 * 384 * SIZE, transcendentals=0
        ),
    )(edge, behind, here, ahead, cot, weights, *after)


def round_kernel(total, *refs):
    refs[-1][...] = total[...].astype(BF16)


def rounded(total, *after):
    return pl.pallas_call(
        round_kernel,
        in_specs=[pl.BlockSpec(memory_space=pltpu.VMEM)]
        + [pl.BlockSpec(memory_space=pl.ANY)] * len(after),
        out_shape=jax.ShapeDtypeStruct(total.shape, BF16),
        compiler_params=params(),
    )(total, *after)


def pick(array, index, axis):
    return lax.dynamic_index_in_dim(array, index, axis, keepdims=False)


def add_kernel(half, own, received, mine, theirs):
    mine[...] = (own[half[0]] + received[half[0]]).astype(BF16)
    theirs[...] = (own[1 - half[0]] + received[1 - half[0]]).astype(BF16)


def add_cores(half, own, received):
    vmem = pl.BlockSpec(memory_space=pltpu.VMEM)
    return pl.pallas_call(
        add_kernel,
        in_specs=[pl.BlockSpec(memory_space=pltpu.SMEM), vmem, vmem],
        out_specs=[vmem, vmem],
        out_shape=[jax.ShapeDtypeStruct((96, 1664), BF16)] * 2,
        compiler_params=params(),
    )(half.reshape(1), own, received)


def sum_in_column(own, given):
    own, theirs = add_cores(lax.axis_index("ch"), own, send(given, other_core))
    beside = send(own, other_low).astype(F32)
    across = send(theirs, other_ch).astype(F32)
    third = send(theirs, other_both).astype(F32)
    return ((own.astype(F32) + beside) + (across + third)).reshape(4, 24, 1664)


def place_on_z():
    return (lax.axis_index("seq") >> 3) & 3


def scatter_over_z(mine):
    z = place_on_z()
    total = pick(mine, z, 0)
    for k in (1, 2, 3):
        part = pick(mine, z ^ k, 0).astype(BF16)
        total = total + send(part, flip(8 * k)).astype(F32)
    return total


def add_flips(own, a, b):
    first, second, third = (send(own, flip(m)).astype(F32) for m in (a, b, a ^ b))
    return (own.astype(F32) + first) + (second + third)


def place_kernel(z, *refs):
    out = refs[-1]
    for k in range(4):
        out[pl.ds(z[0] ^ k, 1)] = refs[k][...][None]


def gather_over_z(total, *after):
    found = [total] + [send(total, flip(8 * k)) for k in (1, 2, 3)]
    return pl.pallas_call(
        place_kernel,
        in_specs=[pl.BlockSpec(memory_space=pltpu.SMEM)]
        + [pl.BlockSpec(memory_space=pltpu.VMEM)] * 4
        + [pl.BlockSpec(memory_space=pl.ANY)] * len(after),
        out_shape=jax.ShapeDtypeStruct((4, 24, 1664), BF16),
        compiler_params=params(),
    )(place_on_z().reshape(1), *found, *after)


def result_kernel(core, own, across, taps, mix, bias):
    for source, base in ((own, 96 * core[0]), (across, 96 * (1 - core[0]))):
        for j in range(4):
            place = pl.ds(pl.multiple_of(base + 24 * j, 8), 24)
            block = source[j].astype(F32)
            for k in range(3):
                taps[k, place, :] = block[:, 384 * k : 384 * (k + 1)]
            mix[place, :] = block[:, 1152:1536]
            bias[place, :] = block[:, 1536:1664]


def results(gathered):
    core = (lax.axis_index("seq") & 1).reshape(1)
    vmem = pl.BlockSpec(memory_space=pltpu.VMEM)
    taps, mix, bias = pl.pallas_call(
        result_kernel,
        in_specs=[pl.BlockSpec(memory_space=pltpu.SMEM), vmem, vmem],
        out_specs=[vmem] * 3,
        out_shape=[
            jax.ShapeDtypeStruct((3, 192, 384), F32),
            jax.ShapeDtypeStruct((192, 384), F32),
            jax.ShapeDtypeStruct((192, 128), F32),
        ],
        compiler_params=params(),
    )(core, gathered, send(gathered, other_core))
    return taps, bias[:, 0], mix


def edges(chip, core):
    first, final = (chip == 0).astype(jnp.int32), (chip == 31).astype(jnp.int32)
    one, zero = jnp.int32(1), jnp.int32(0)
    return jnp.stack([zero, 1 - first, 1 - first, one, final, one, one, 1 - final, core])


def per_device(inputs, convolution_weight, conv_bias, mix_weight, cotangent):
    factor = 1.0 / math.sqrt(inputs.shape[0] * inputs.shape[2] * lax.axis_size("seq"))
    edge = edges((lax.axis_index("seq") >> 1) & 31, lax.axis_index("seq") & 1)
    field = (2, 2, 192, SIZE)
    column = jnp.stack([lax.axis_index("ch"), lax.axis_index("seq") >> 6]).astype(jnp.int32)
    here = [gather_column(inputs, column, k) for k in range(CHUNKS)]
    weights = pack_weights(convolution_weight, mix_weight, conv_bias, here[-1])
    weights = gather_weights(weights, lax.axis_index("ch"), lax.axis_index("seq") & 1)
    cot = [exchange(pack(cotangent, k, weights)).reshape(field) for k in range(CHUNKS)]
    sides = [(send(a, chips_on(1)), send(a, chips_on(-1))) for a in here]
    sums, acts, grads, grad_sides = (), [], [], []
    for k in range(CHUNKS):
        act, grad, *sums = middle(edge, sides[k][0], here[k], sides[k][1], cot[k], weights)
        acts.append(act)
        grads.append(grad)
        grad_sides.append((send(grad, chips_on(1)), send(grad, chips_on(-1))))

    def flat(piece):
        return piece.reshape(4, 192, SIZE)

    mine = sum_in_column(*sums)
    outs = [exchange(flat(mixed(edge, here[k], acts[k], weights))) for k in range(CHUNKS)]
    total = scatter_over_z(mine).astype(BF16)
    input_grads = [
        back(edge, grad_sides[k][0], grads[k], grad_sides[k][1], cot[k], weights, *outs, total)
        for k in range(CHUNKS)
    ]
    input_parts = [exchange(flat(p)) for p in input_grads]
    outputs, input_grad = unpack(outs), unpack(input_parts)
    total = total.astype(F32) + send(total, flip(32)).astype(F32)
    total = add_flips(rounded(total, *input_grads), 2, 4)
    gathered = gather_over_z((total * factor).astype(BF16))
    weight_grad, bias_grad, mix_grad = results(gathered)
    return outputs, input_grad, weight_grad, bias_grad, mix_grad


def solution(mesh):
    in_specs = (
        P(None, "ch", "seq"),
        P(None, "ch", None),
        P("ch"),
        P("ch", None),
        P(None, "ch", "seq"),
    )
    out_specs = (
        P(None, "ch", "seq"),
        P(None, "ch", "seq"),
        P(None, "ch", None),
        P("ch"),
        P("ch", None),
    )
    return jax.shard_map(
        per_device, mesh=mesh, in_specs=in_specs, out_specs=out_specs, check_vma=False
    )
```

```python
import math

import jax
import jax.numpy as jnp
from jax import lax
from jax.experimental import pallas as pl
from jax.experimental.pallas import tpu as pltpu
from jax.sharding import PartitionSpec as P

BF16, F32 = jnp.bfloat16, jnp.float32
AXES = ("seq", "ch")
CHUNKS = 1
SIZE = 1024 // CHUNKS
TILE = 1024
ROOT = math.sqrt(2.0 / math.pi)
CUBE = 0.044715


def route(target):
    pairs = []
    for s in range(128):
        for h in range(2):
            to = target(s, h)
            pairs.append((2 * s + h, 2 * to[0] + to[1]))
    return pairs


def send(block, target):
    return lax.ppermute(block, AXES, route(target))


def other_ch(s, h):
    return s, 1 - h


def other_core(s, h):
    return s ^ 1, h


def flip(bits):
    return lambda s, h: (s ^ bits, h)


def chips_on(step):
    return lambda s, h: ((s & 64) | ((s + (2 - 4 * (s & 1)) * step) & 63), h)


def column_groups():
    return [[2 * (64 * (y & 1) + place) + (y >> 1) for y in range(4)] for place in range(64)]


def exchange(block):
    return lax.all_to_all(block, AXES, 0, 0, axis_index_groups=column_groups())


def dot(a, b, dims=((1,), (0,))):
    return lax.dot_general(a, b, (dims, ((), ())), preferred_element_type=F32)


def params(megabytes=28):
    return pltpu.CompilerParams(vmem_limit_bytes=megabytes * 2**20)


def copy_kernel(source, *refs):
    refs[-1][...] = source[...]


def pack(array, k, *after):
    block = (1, 192, SIZE)
    return pl.pallas_call(
        copy_kernel,
        grid=(4,),
        in_specs=[pl.BlockSpec(block, lambda d: (d // 2, 0, (d % 2) * CHUNKS + k))]
        + [pl.BlockSpec(memory_space=pl.ANY)] * len(after),
        out_specs=pl.BlockSpec(block, lambda d: (d, 0, 0)),
        out_shape=jax.ShapeDtypeStruct((4, 192, SIZE), BF16),
        compiler_params=params(),
        cost_estimate=pl.CostEstimate(flops=0, bytes_accessed=16 * 192 * SIZE, transcendentals=0),
    )(array, *after)


def split_kernel(place, *refs):
    for source, target in zip(refs[:4], refs[4:]):
        target[...] = source[0]


def split(array, place, k):
    def source(other_half, other_low):
        def index(i, place):
            half, low = place[0] ^ other_half, place[1] ^ other_low
            return half, 0, low * CHUNKS + k

        return pl.BlockSpec((1, 192, SIZE), index)

    plain = pl.BlockSpec((192, SIZE), lambda i, place: (0, 0))
    return pl.pallas_call(
        split_kernel,
        grid_spec=pltpu.PrefetchScalarGridSpec(
            num_scalar_prefetch=1,
            grid=(1,),
            in_specs=[source(0, 0), source(0, 1), source(1, 0), source(1, 1)],
            out_specs=[plain] * 4,
        ),
        out_shape=[jax.ShapeDtypeStruct((192, SIZE), BF16)] * 4,
        compiler_params=params(),
    )(place, array, array, array, array)


def join_kernel(place, own, low, half, both, out):
    for source, a, b in ((own, 0, 0), (low, 0, 1), (half, 1, 0), (both, 1, 1)):
        out[pl.ds(place[0] ^ a, 1), pl.ds(place[1] ^ b, 1)] = source[...][None, None]


def join(place, *parts):
    vmem = pl.BlockSpec(memory_space=pltpu.VMEM)
    return pl.pallas_call(
        join_kernel,
        in_specs=[pl.BlockSpec(memory_space=pltpu.SMEM)] + [vmem] * 4,
        out_specs=vmem,
        out_shape=jax.ShapeDtypeStruct((2, 2, 192, SIZE), BF16),
        compiler_params=params(),
    )(place, *parts)


def other_low(s, h):
    return s ^ 64, h


def other_both(s, h):
    return s ^ 64, 1 - h


def gather_column(array, place, k):
    own, low, half, both = split(array, place, k)
    return join(place, own, send(low, other_low), send(half, other_ch), send(both, other_both))


def unpack_kernel(source, target, token):
    target[0, :, 0:1024] = source[0]
    target[0, :, 1024:2048] = source[1]
    token[...] = jnp.zeros((8, 128), F32)


def unpack(pieces):
    return pl.pallas_call(
        unpack_kernel,
        grid=(2,),
        in_specs=[pl.BlockSpec((2, 192, 1024), lambda d: (d, 0, 0))],
        out_specs=[
            pl.BlockSpec((1, 192, 2048), lambda d: (d, 0, 0)),
            pl.BlockSpec((8, 128), lambda d: (0, 0)),
        ],
        out_shape=[
            jax.ShapeDtypeStruct((2, 192, 2048), BF16),
            jax.ShapeDtypeStruct((8, 128), F32),
        ],
        compiler_params=params(),
        cost_estimate=pl.CostEstimate(flops=0, bytes_accessed=16 * 192 * 1024, transcendentals=0),
    )(pieces[0])


def weights_kernel(taps, mix, bias, *refs):
    out = refs[-1]
    for k in range(3):
        out[:, 384 * k : 384 * (k + 1)] = taps[k]
    out[:, 1152:1536] = mix[...]
    value = jnp.broadcast_to(bias[...], (192, 128))
    high = value.astype(BF16).astype(F32)
    middle = (value - high).astype(BF16).astype(F32)
    low = value - high - middle
    lane = lax.broadcasted_iota(jnp.int32, (192, 128), 1)
    split = jnp.where(lane == 0, high, jnp.where(lane == 1, middle, jnp.where(lane == 2, low, 0.0)))
    out[:, 1536:1664] = split.astype(BF16)


def pack_weights(taps, mix, bias, *after):
    return pl.pallas_call(
        weights_kernel,
        in_specs=[pl.BlockSpec(memory_space=pltpu.VMEM)] * 3
        + [pl.BlockSpec(memory_space=pl.ANY)] * len(after),
        out_shape=jax.ShapeDtypeStruct((192, 1664), BF16),
        compiler_params=params(),
    )(taps, mix, bias.reshape(192, 1), *after)


def assemble_kernel(place, own, straight, crossed, out):
    half, core = place[0], place[1]
    out[pl.ds(pl.multiple_of(192 * half, 192), 192), :] = own[...]
    base = 192 * (1 - half)
    out[pl.ds(pl.multiple_of(base + 96 * core, 96), 96), :] = straight[...]
    out[pl.ds(pl.multiple_of(base + 96 * (1 - core), 96), 96), :] = crossed[...]


def gather_weights(own, half, core):
    straight = send(pick(own.reshape(2, 96, 1664), core, 0), other_ch)
    crossed = send(straight, other_core)
    return pl.pallas_call(
        assemble_kernel,
        in_specs=[pl.BlockSpec(memory_space=pltpu.SMEM)]
        + [pl.BlockSpec(memory_space=pltpu.VMEM)] * 3,
        out_shape=jax.ShapeDtypeStruct((384, 1664), BF16),
        compiler_params=params(),
    )(jnp.stack([half, core]).astype(jnp.int32), own, straight, crossed)


def rows(ref):
    return ref[...].reshape(384, TILE)


def neighbours(first, second, edge):
    group, core = pl.program_id(0), edge[8]
    first, second = rows(first), rows(second)
    nothing = jnp.zeros((384, TILE), BF16)
    behind = jnp.where(core == 0, first, second)
    ahead = jnp.where(core == 0, second, first)
    behind = jnp.where(edge[2 + group] == 1, behind, nothing)
    return behind, jnp.where(edge[6 + group] == 1, ahead, nothing)


def middle_kernel(edge, first, here, second, cot, weights, *refs):
    act_out, grad_pre, own, theirs, sums = refs
    group = pl.program_id(0)

    @pl.when((group == 0) & (pl.program_id(1) == 0))
    def _():
        sums[...] = jnp.zeros((384, 1664), F32)

    center = rows(here)
    before, after = neighbours(first, second, edge)
    field = jnp.concatenate([before, center, after], axis=0)
    bias = weights[:, 1536:1664].astype(F32)
    bias = bias[:, 0:1] + bias[:, 1:2] + bias[:, 2:3]
    pre = dot(weights[:, 0:1152], field) + bias
    square = pre * pre
    bent = jnp.tanh(ROOT * pre * (1.0 + CUBE * square))
    half = 0.5 * (1.0 + bent)
    act = (pre * half).astype(BF16)
    slope = half + 0.5 * pre * (1.0 - bent * bent) * (ROOT * (1.0 + 3.0 * CUBE * square))
    mix = weights[:, 1152:1536]
    act_out[...] = act.reshape(act_out.shape)
    upstream = rows(cot)
    grad = (dot(mix, upstream, ((0,), (0,))) * slope).astype(BF16)
    grad_pre[...] = grad.reshape(grad_pre.shape)
    last = ((1,), (1,))
    sums[:, 0:1152] += dot(grad, field, last)
    sums[:, 1152:1536] += dot(upstream, act, last)
    sums[:, 1536:1664] += jnp.broadcast_to(
        jnp.sum(grad.astype(F32), axis=1, keepdims=True), (384, 128)
    )

    @pl.when((group == 1) & (pl.program_id(1) == pl.num_programs(1) - 1))
    def _():
        core = edge[8]
        for h in range(2):
            own[h] = sums[pl.ds(pl.multiple_of(192 * h + 96 * core, 96), 96), :]
            theirs[h] = sums[pl.ds(pl.multiple_of(192 * h + 96 * (1 - core), 96), 96), :]


def tile_specs():
    block = (2, 1, 192, TILE)
    plain = pl.BlockSpec(block, lambda g, i, edge: (0, g, 0, i))
    behind = pl.BlockSpec(block, lambda g, i, edge: (0, edge[g], 0, i))
    ahead = pl.BlockSpec(block, lambda g, i, edge: (0, edge[4 + g], 0, i))
    return plain, behind, ahead


def whole(array):
    return pl.BlockSpec(array.shape, lambda g, i, edge: (0,) * array.ndim)


def middle(edge, behind, here, ahead, cot, weights):
    plain, before, after = tile_specs()
    sums = jax.ShapeDtypeStruct((2, 96, 1664), F32)
    field = jax.ShapeDtypeStruct((2, 2, 192, SIZE), BF16)
    return pl.pallas_call(
        middle_kernel,
        grid_spec=pltpu.PrefetchScalarGridSpec(
            num_scalar_prefetch=1,
            grid=(2, SIZE // TILE),
            in_specs=[before, plain, after, plain, whole(weights)],
            out_specs=[plain, plain, whole(sums), whole(sums)],
            scratch_shapes=[pltpu.VMEM((384, 1664), F32)],
        ),
        out_shape=[field, field, sums, sums],
        compiler_params=params(),
        cost_estimate=pl.CostEstimate(
            flops=36 * 384 * 384 * SIZE, bytes_accessed=24 * 384 * SIZE, transcendentals=768 * SIZE
        ),
    )(edge, behind, here, ahead, cot, weights)


def mix_kernel(edge, here, act, weights, *refs):
    out, taps = refs[-2:]

    @pl.when((pl.program_id(0) == 0) & (pl.program_id(1) == 0))
    def _():
        for k in range(3):
            tap = weights[:, 384 * (2 - k) : 384 * (3 - k)]
            taps[:, 384 * k : 384 * (k + 1)] = tap.T

    result = rows(here).astype(F32) + dot(weights[:, 1152:1536], rows(act))
    out[...] = result.astype(BF16).reshape(out.shape)


def mixed(edge, here, act, weights, *after):
    plain, _, _ = tile_specs()
    return pl.pallas_call(
        mix_kernel,
        grid_spec=pltpu.PrefetchScalarGridSpec(
            num_scalar_prefetch=1,
            grid=(2, SIZE // TILE),
            in_specs=[plain, plain, whole(weights)]
            + [pl.BlockSpec(memory_space=pl.ANY)] * len(after),
            out_specs=[plain, pl.BlockSpec((384, 1152), lambda g, i, edge: (0, 0))],
        ),
        out_shape=[
            pltpu.HBM((2, 2, 192, SIZE), BF16),
            jax.ShapeDtypeStruct((384, 1152), BF16),
        ],
        compiler_params=params(),
        cost_estimate=pl.CostEstimate(
            flops=4 * 384 * 384 * SIZE, bytes_accessed=12 * 384 * SIZE, transcendentals=0
        ),
    )(edge, here, act, weights, *after)


def back_kernel(edge, first, here, second, cot, taps, *refs):
    out, token = refs[-2:]
    token[...] = jnp.zeros((8, 128), F32)
    before, after = neighbours(first, second, edge)
    field = jnp.concatenate([before, rows(here), after], axis=0)
    result = (rows(cot).astype(F32) + dot(taps[...], field)).astype(BF16)
    out[...] = result.reshape(out.shape)


def back(edge, behind, here, ahead, cot, taps, *after):
    plain, before, beyond = tile_specs()
    return pl.pallas_call(
        back_kernel,
        grid_spec=pltpu.PrefetchScalarGridSpec(
            num_scalar_prefetch=1,
            grid=(2, SIZE // TILE),
            in_specs=[before, plain, beyond, plain, whole(taps)]
            + [pl.BlockSpec(memory_space=pl.ANY)] * len(after),
            out_specs=[plain, pl.BlockSpec((8, 128), lambda g, i, edge: (0, 0))],
        ),
        out_shape=[
            pltpu.HBM((2, 2, 192, SIZE), BF16),
            jax.ShapeDtypeStruct((8, 128), F32),
        ],
        compiler_params=params(),
        cost_estimate=pl.CostEstimate(
            flops=12 * 384 * 384 * SIZE, bytes_accessed=20 * 384 * SIZE, transcendentals=0
        ),
    )(edge, behind, here, ahead, cot, taps, *after)


def round_kernel(total, *refs):
    refs[-1][...] = total[...].astype(BF16)


def rounded(total, *after):
    return pl.pallas_call(
        round_kernel,
        in_specs=[pl.BlockSpec(memory_space=pltpu.VMEM)]
        + [pl.BlockSpec(memory_space=pl.ANY)] * len(after),
        out_shape=jax.ShapeDtypeStruct(total.shape, BF16),
        compiler_params=params(),
    )(total, *after)


def pick(array, index, axis):
    return lax.dynamic_index_in_dim(array, index, axis, keepdims=False)


def add_kernel(half, own, received, mine, theirs):
    mine[...] = (own[half[0]] + received[half[0]]).astype(BF16)
    theirs[...] = (own[1 - half[0]] + received[1 - half[0]]).astype(BF16)


def add_cores(half, own, received):
    vmem = pl.BlockSpec(memory_space=pltpu.VMEM)
    return pl.pallas_call(
        add_kernel,
        in_specs=[pl.BlockSpec(memory_space=pltpu.SMEM), vmem, vmem],
        out_specs=[vmem, vmem],
        out_shape=[jax.ShapeDtypeStruct((96, 1664), BF16)] * 2,
        compiler_params=params(),
    )(half.reshape(1), own, received)


def sum_in_column(own, given):
    own, theirs = add_cores(lax.axis_index("ch"), own, send(given, other_core))
    beside = send(own, other_low).astype(F32)
    across = send(theirs, other_ch).astype(F32)
    third = send(theirs, other_both).astype(F32)
    return ((own.astype(F32) + beside) + (across + third)).reshape(4, 24, 1664)


def place_on_z():
    return (lax.axis_index("seq") >> 3) & 3


def scatter_over_z(mine):
    z = place_on_z()
    total = pick(mine, z, 0)
    for k in (1, 2, 3):
        part = pick(mine, z ^ k, 0).astype(BF16)
        total = total + send(part, flip(8 * k)).astype(F32)
    return total


def add_flips(own, a, b):
    first, second, third = (send(own, flip(m)).astype(F32) for m in (a, b, a ^ b))
    return (own.astype(F32) + first) + (second + third)


def place_kernel(z, *refs):
    out = refs[-1]
    for k in range(4):
        out[pl.ds(z[0] ^ k, 1)] = refs[k][...][None]


def gather_over_z(total, *after):
    found = [total] + [send(total, flip(8 * k)) for k in (1, 2, 3)]
    return pl.pallas_call(
        place_kernel,
        in_specs=[pl.BlockSpec(memory_space=pltpu.SMEM)]
        + [pl.BlockSpec(memory_space=pltpu.VMEM)] * 4
        + [pl.BlockSpec(memory_space=pl.ANY)] * len(after),
        out_shape=jax.ShapeDtypeStruct((4, 24, 1664), BF16),
        compiler_params=params(),
    )(place_on_z().reshape(1), *found, *after)


def result_kernel(core, own, across, taps, mix, bias):
    for source, base in ((own, 96 * core[0]), (across, 96 * (1 - core[0]))):
        for j in range(4):
            place = pl.ds(pl.multiple_of(base + 24 * j, 8), 24)
            block = source[j].astype(F32)
            for k in range(3):
                taps[k, place, :] = block[:, 384 * k : 384 * (k + 1)]
            mix[place, :] = block[:, 1152:1536]
            bias[place, :] = block[:, 1536:1664]


def results(gathered):
    core = (lax.axis_index("seq") & 1).reshape(1)
    vmem = pl.BlockSpec(memory_space=pltpu.VMEM)
    taps, mix, bias = pl.pallas_call(
        result_kernel,
        in_specs=[pl.BlockSpec(memory_space=pltpu.SMEM), vmem, vmem],
        out_specs=[vmem] * 3,
        out_shape=[
            jax.ShapeDtypeStruct((3, 192, 384), F32),
            jax.ShapeDtypeStruct((192, 384), F32),
            jax.ShapeDtypeStruct((192, 128), F32),
        ],
        compiler_params=params(),
    )(core, gathered, send(gathered, other_core))
    return taps, bias[:, 0], mix


def edges(chip, core):
    first, final = (chip == 0).astype(jnp.int32), (chip == 31).astype(jnp.int32)
    one, zero = jnp.int32(1), jnp.int32(0)
    behind, ahead = jnp.stack([zero, 1 - first]), jnp.stack([final, one])
    return jnp.concatenate(
        [
            jnp.where(core == 0, behind, ahead),
            jnp.stack([1 - first, one]),
            jnp.where(core == 0, ahead, behind),
            jnp.stack([one, 1 - final, core]),
        ]
    )


def per_device(inputs, convolution_weight, conv_bias, mix_weight, cotangent):
    factor = 1.0 / math.sqrt(inputs.shape[0] * inputs.shape[2] * lax.axis_size("seq"))
    edge = edges((lax.axis_index("seq") >> 1) & 31, lax.axis_index("seq") & 1)
    field = (2, 2, 192, SIZE)
    column = jnp.stack([lax.axis_index("ch"), lax.axis_index("seq") >> 6]).astype(jnp.int32)
    here = [gather_column(inputs, column, k) for k in range(CHUNKS)]
    weights = pack_weights(convolution_weight, mix_weight, conv_bias, here[-1])
    weights = gather_weights(weights, lax.axis_index("ch"), lax.axis_index("seq") & 1)
    cot = [exchange(pack(cotangent, k, weights)).reshape(field) for k in range(CHUNKS)]
    sides = [(send(a, chips_on(1)), send(a, chips_on(-1))) for a in here]
    sums, acts, grads, grad_sides = (), [], [], []
    for k in range(CHUNKS):
        act, grad, *sums = middle(edge, sides[k][0], here[k], sides[k][1], cot[k], weights)
        acts.append(act)
        grads.append(grad)
        grad_sides.append((send(grad, chips_on(1)), send(grad, chips_on(-1))))

    def flat(piece):
        return piece.reshape(4, 192, SIZE)

    mine = sum_in_column(*sums)
    out, taps = mixed(edge, here[0], acts[0], weights)
    outs = [exchange(flat(out))]
    total = scatter_over_z(mine).astype(BF16)
    input_grads = [
        back(edge, grad_sides[k][0], grads[k], grad_sides[k][1], cot[k], taps, *outs, total)
        for k in range(CHUNKS)
    ]
    input_parts = [exchange(flat(p)) for p, _ in input_grads]
    outputs, _ = unpack(outs)
    input_grad, unpacked = unpack(input_parts)
    total = total.astype(F32) + send(total, flip(32)).astype(F32)
    total = add_flips(rounded(total, *[token for _, token in input_grads]), 2, 4)
    gathered = gather_over_z((total * factor).astype(BF16), unpacked)
    weight_grad, bias_grad, mix_grad = results(gathered)
    return outputs, input_grad, weight_grad, bias_grad, mix_grad


def solution(mesh):
    in_specs = (
        P(None, "ch", "seq"),
        P(None, "ch", None),
        P("ch"),
        P("ch", None),
        P(None, "ch", "seq"),
    )
    out_specs = (
        P(None, "ch", "seq"),
        P(None, "ch", "seq"),
        P(None, "ch", None),
        P("ch"),
        P("ch", None),
    )
    return jax.shard_map(
        per_device, mesh=mesh, in_specs=in_specs, out_specs=out_specs, check_vma=False
    )
```

```python
import math

import jax
import jax.numpy as jnp
from jax import lax
from jax.experimental import pallas as pl
from jax.experimental.pallas import tpu as pltpu
from jax.sharding import PartitionSpec as P

BF16, F32 = jnp.bfloat16, jnp.float32
AXES = ("seq", "ch")
CHUNKS = 1
SIZE = 1024 // CHUNKS
TILE = 1024
ROOT = math.sqrt(2.0 / math.pi)
CUBE = 0.044715


def route(target):
    pairs = []
    for s in range(128):
        for h in range(2):
            to = target(s, h)
            pairs.append((2 * s + h, 2 * to[0] + to[1]))
    return pairs


def send(block, target):
    return lax.ppermute(block, AXES, route(target))


def other_ch(s, h):
    return s, 1 - h


def other_core(s, h):
    return s ^ 1, h


def flip(bits):
    return lambda s, h: (s ^ bits, h)


def chips_on(step):
    return lambda s, h: ((s & 64) | ((s + (2 - 4 * (s & 1)) * step) & 63), h)


def column_groups():
    return [[2 * (64 * (y & 1) + place) + (y >> 1) for y in range(4)] for place in range(64)]


def exchange(block):
    return lax.all_to_all(block, AXES, 0, 0, axis_index_groups=column_groups())


def dot(a, b, dims=((1,), (0,))):
    return lax.dot_general(a, b, (dims, ((), ())), preferred_element_type=F32)


def params(megabytes=28):
    return pltpu.CompilerParams(vmem_limit_bytes=megabytes * 2**20)


def copy_kernel(source, *refs):
    refs[-1][...] = source[...]


def pack(array, k, *after):
    block = (1, 192, SIZE)
    return pl.pallas_call(
        copy_kernel,
        grid=(4,),
        in_specs=[pl.BlockSpec(block, lambda d: (d // 2, 0, (d % 2) * CHUNKS + k))]
        + [pl.BlockSpec(memory_space=pl.ANY)] * len(after),
        out_specs=pl.BlockSpec(block, lambda d: (d, 0, 0)),
        out_shape=jax.ShapeDtypeStruct((4, 192, SIZE), BF16),
        compiler_params=params(),
        cost_estimate=pl.CostEstimate(flops=0, bytes_accessed=16 * 192 * SIZE, transcendentals=0),
    )(array, *after)


def split_kernel(place, *refs):
    for source, target in zip(refs[:4], refs[4:]):
        target[...] = source[0]


def split(array, place, k):
    def source(other_half, other_low):
        def index(i, place):
            half, low = place[0] ^ other_half, place[1] ^ other_low
            return half, 0, low * CHUNKS + k

        return pl.BlockSpec((1, 192, SIZE), index)

    plain = pl.BlockSpec((192, SIZE), lambda i, place: (0, 0))
    return pl.pallas_call(
        split_kernel,
        grid_spec=pltpu.PrefetchScalarGridSpec(
            num_scalar_prefetch=1,
            grid=(1,),
            in_specs=[source(0, 0), source(0, 1), source(1, 0), source(1, 1)],
            out_specs=[plain] * 4,
        ),
        out_shape=[jax.ShapeDtypeStruct((192, SIZE), BF16)] * 4,
        compiler_params=params(),
    )(place, array, array, array, array)


def join_kernel(place, own, low, half, both, out):
    for source, a, b in ((own, 0, 0), (low, 0, 1), (half, 1, 0), (both, 1, 1)):
        out[pl.ds(place[0] ^ a, 1), pl.ds(place[1] ^ b, 1)] = source[...][None, None]


def join(place, *parts):
    vmem = pl.BlockSpec(memory_space=pltpu.VMEM)
    return pl.pallas_call(
        join_kernel,
        in_specs=[pl.BlockSpec(memory_space=pltpu.SMEM)] + [vmem] * 4,
        out_specs=vmem,
        out_shape=jax.ShapeDtypeStruct((2, 2, 192, SIZE), BF16),
        compiler_params=params(),
    )(place, *parts)


def other_low(s, h):
    return s ^ 64, h


def other_both(s, h):
    return s ^ 64, 1 - h


def gather_column(array, place, k):
    own, low, half, both = split(array, place, k)
    return join(place, own, send(low, other_low), send(half, other_ch), send(both, other_both))


def unpack_kernel(source, target, token):
    target[0, :, 0:1024] = source[0]
    target[0, :, 1024:2048] = source[1]
    token[...] = jnp.zeros((8, 128), F32)


def unpack(pieces):
    return pl.pallas_call(
        unpack_kernel,
        grid=(2,),
        in_specs=[pl.BlockSpec((2, 192, 1024), lambda d: (d, 0, 0))],
        out_specs=[
            pl.BlockSpec((1, 192, 2048), lambda d: (d, 0, 0)),
            pl.BlockSpec((8, 128), lambda d: (0, 0)),
        ],
        out_shape=[
            jax.ShapeDtypeStruct((2, 192, 2048), BF16),
            jax.ShapeDtypeStruct((8, 128), F32),
        ],
        compiler_params=params(),
        cost_estimate=pl.CostEstimate(flops=0, bytes_accessed=16 * 192 * 1024, transcendentals=0),
    )(pieces[0])


def weights_kernel(taps, mix, bias, *refs):
    out = refs[-1]
    for k in range(3):
        out[:, 384 * k : 384 * (k + 1)] = taps[k]
    out[:, 1152:1536] = mix[...]
    value = jnp.broadcast_to(bias[...], (192, 128))
    high = value.astype(BF16).astype(F32)
    middle = (value - high).astype(BF16).astype(F32)
    low = value - high - middle
    lane = lax.broadcasted_iota(jnp.int32, (192, 128), 1)
    split = jnp.where(lane == 0, high, jnp.where(lane == 1, middle, jnp.where(lane == 2, low, 0.0)))
    out[:, 1536:1664] = split.astype(BF16)


def pack_weights(taps, mix, bias, *after):
    return pl.pallas_call(
        weights_kernel,
        in_specs=[pl.BlockSpec(memory_space=pltpu.VMEM)] * 3
        + [pl.BlockSpec(memory_space=pl.ANY)] * len(after),
        out_shape=jax.ShapeDtypeStruct((192, 1664), BF16),
        compiler_params=params(),
    )(taps, mix, bias.reshape(192, 1), *after)


def assemble_kernel(place, own, straight, crossed, out):
    half, core = place[0], place[1]
    out[pl.ds(pl.multiple_of(192 * half, 192), 192), :] = own[...]
    base = 192 * (1 - half)
    out[pl.ds(pl.multiple_of(base + 96 * core, 96), 96), :] = straight[...]
    out[pl.ds(pl.multiple_of(base + 96 * (1 - core), 96), 96), :] = crossed[...]


def gather_weights(own, half, core):
    straight = send(pick(own.reshape(2, 96, 1664), core, 0), other_ch)
    crossed = send(straight, other_core)
    return pl.pallas_call(
        assemble_kernel,
        in_specs=[pl.BlockSpec(memory_space=pltpu.SMEM)]
        + [pl.BlockSpec(memory_space=pltpu.VMEM)] * 3,
        out_shape=jax.ShapeDtypeStruct((384, 1664), BF16),
        compiler_params=params(),
    )(jnp.stack([half, core]).astype(jnp.int32), own, straight, crossed)


def rows(ref):
    return ref[...].reshape(384, TILE)


def neighbours(first, second, edge):
    group, core = pl.program_id(0), edge[8]
    first, second = rows(first), rows(second)
    nothing = jnp.zeros((384, TILE), BF16)
    behind = jnp.where(core == 0, first, second)
    ahead = jnp.where(core == 0, second, first)
    behind = jnp.where(edge[2 + group] == 1, behind, nothing)
    return behind, jnp.where(edge[6 + group] == 1, ahead, nothing)


def middle_kernel(edge, first, here, second, cot, weights, *refs):
    act_out, grad_pre, own, theirs, sums = refs
    group = pl.program_id(0)

    @pl.when((group == 0) & (pl.program_id(1) == 0))
    def _():
        sums[...] = jnp.zeros((384, 1664), F32)

    center = rows(here)
    before, after = neighbours(first, second, edge)
    field = jnp.concatenate([before, center, after], axis=0)
    bias = weights[:, 1536:1664].astype(F32)
    bias = bias[:, 0:1] + bias[:, 1:2] + bias[:, 2:3]
    pre = dot(weights[:, 0:1152], field) + bias
    square = pre * pre
    bent = jnp.tanh(ROOT * pre * (1.0 + CUBE * square))
    half = 0.5 * (1.0 + bent)
    act = (pre * half).astype(BF16)
    slope = half + 0.5 * pre * (1.0 - bent * bent) * (ROOT * (1.0 + 3.0 * CUBE * square))
    mix = weights[:, 1152:1536]
    act_out[...] = act.reshape(act_out.shape)
    upstream = rows(cot)
    grad = (dot(mix, upstream, ((0,), (0,))) * slope).astype(BF16)
    grad_pre[...] = grad.reshape(grad_pre.shape)
    last = ((1,), (1,))
    sums[:, 0:1152] += dot(grad, field, last)
    sums[:, 1152:1536] += dot(upstream, act, last)
    sums[:, 1536:1664] += jnp.broadcast_to(
        jnp.sum(grad.astype(F32), axis=1, keepdims=True), (384, 128)
    )

    @pl.when((group == 1) & (pl.program_id(1) == pl.num_programs(1) - 1))
    def _():
        core = edge[8]
        for h in range(2):
            own[h] = sums[pl.ds(pl.multiple_of(192 * h + 96 * core, 96), 96), :]
            theirs[h] = sums[pl.ds(pl.multiple_of(192 * h + 96 * (1 - core), 96), 96), :]


def tile_specs():
    block = (2, 1, 192, TILE)
    plain = pl.BlockSpec(block, lambda g, i, edge: (0, g, 0, i))
    behind = pl.BlockSpec(block, lambda g, i, edge: (0, edge[g], 0, i))
    ahead = pl.BlockSpec(block, lambda g, i, edge: (0, edge[4 + g], 0, i))
    return plain, behind, ahead


def whole(array):
    return pl.BlockSpec(array.shape, lambda g, i, edge: (0,) * array.ndim)


def middle(edge, behind, here, ahead, cot, weights):
    plain, before, after = tile_specs()
    sums = jax.ShapeDtypeStruct((2, 96, 1664), F32)
    field = jax.ShapeDtypeStruct((2, 2, 192, SIZE), BF16)
    return pl.pallas_call(
        middle_kernel,
        grid_spec=pltpu.PrefetchScalarGridSpec(
            num_scalar_prefetch=1,
            grid=(2, SIZE // TILE),
            in_specs=[before, plain, after, plain, whole(weights)],
            out_specs=[plain, plain, whole(sums), whole(sums)],
            scratch_shapes=[pltpu.VMEM((384, 1664), F32)],
        ),
        out_shape=[field, field, sums, sums],
        compiler_params=params(),
        cost_estimate=pl.CostEstimate(
            flops=36 * 384 * 384 * SIZE, bytes_accessed=24 * 384 * SIZE, transcendentals=768 * SIZE
        ),
    )(edge, behind, here, ahead, cot, weights)


def mix_kernel(edge, here, act, weights, *refs):
    out, taps = refs[-2:]

    @pl.when((pl.program_id(0) == 0) & (pl.program_id(1) == 0))
    def _():
        for k in range(3):
            tap = weights[:, 384 * (2 - k) : 384 * (3 - k)]
            taps[:, 384 * k : 384 * (k + 1)] = tap.T

    result = rows(here).astype(F32) + dot(weights[:, 1152:1536], rows(act))
    out[...] = result.astype(BF16).reshape(out.shape)


def mixed(edge, here, act, weights, *after):
    plain, _, _ = tile_specs()
    return pl.pallas_call(
        mix_kernel,
        grid_spec=pltpu.PrefetchScalarGridSpec(
            num_scalar_prefetch=1,
            grid=(2, SIZE // TILE),
            in_specs=[plain, plain, whole(weights)]
            + [pl.BlockSpec(memory_space=pl.ANY)] * len(after),
            out_specs=[plain, pl.BlockSpec((384, 1152), lambda g, i, edge: (0, 0))],
        ),
        out_shape=[
            pltpu.HBM((2, 2, 192, SIZE), BF16),
            jax.ShapeDtypeStruct((384, 1152), BF16),
        ],
        compiler_params=params(),
        cost_estimate=pl.CostEstimate(
            flops=4 * 384 * 384 * SIZE, bytes_accessed=12 * 384 * SIZE, transcendentals=0
        ),
    )(edge, here, act, weights, *after)


def back_kernel(edge, first, here, second, cot, taps, *refs):
    out, token = refs[-2:]
    token[...] = jnp.zeros((8, 128), F32)
    before, after = neighbours(first, second, edge)
    field = jnp.concatenate([before, rows(here), after], axis=0)
    result = (rows(cot).astype(F32) + dot(taps[...], field)).astype(BF16)
    out[...] = result.reshape(out.shape)


def back(edge, behind, here, ahead, cot, taps, *after):
    plain, before, beyond = tile_specs()
    return pl.pallas_call(
        back_kernel,
        grid_spec=pltpu.PrefetchScalarGridSpec(
            num_scalar_prefetch=1,
            grid=(2, SIZE // TILE),
            in_specs=[before, plain, beyond, plain, whole(taps)]
            + [pl.BlockSpec(memory_space=pl.ANY)] * len(after),
            out_specs=[plain, pl.BlockSpec((8, 128), lambda g, i, edge: (0, 0))],
        ),
        out_shape=[
            pltpu.HBM((2, 2, 192, SIZE), BF16),
            jax.ShapeDtypeStruct((8, 128), F32),
        ],
        compiler_params=params(),
        cost_estimate=pl.CostEstimate(
            flops=12 * 384 * 384 * SIZE, bytes_accessed=20 * 384 * SIZE, transcendentals=0
        ),
    )(edge, behind, here, ahead, cot, taps, *after)


def round_kernel(total, *refs):
    refs[-1][...] = total[...].astype(BF16)


def rounded(total, *after):
    return pl.pallas_call(
        round_kernel,
        in_specs=[pl.BlockSpec(memory_space=pltpu.VMEM)]
        + [pl.BlockSpec(memory_space=pl.ANY)] * len(after),
        out_shape=jax.ShapeDtypeStruct(total.shape, BF16),
        compiler_params=params(),
    )(total, *after)


def pick(array, index, axis):
    return lax.dynamic_index_in_dim(array, index, axis, keepdims=False)


def add_kernel(half, own, received, mine, theirs):
    mine[...] = (own[half[0]] + received[half[0]]).astype(BF16)
    theirs[...] = (own[1 - half[0]] + received[1 - half[0]]).astype(BF16)


def add_cores(half, own, received):
    vmem = pl.BlockSpec(memory_space=pltpu.VMEM)
    return pl.pallas_call(
        add_kernel,
        in_specs=[pl.BlockSpec(memory_space=pltpu.SMEM), vmem, vmem],
        out_specs=[vmem, vmem],
        out_shape=[jax.ShapeDtypeStruct((96, 1664), BF16)] * 2,
        compiler_params=params(),
    )(half.reshape(1), own, received)


def sum_in_column(own, theirs):
    beside = send(own, other_low).astype(F32)
    across = send(theirs, other_ch).astype(F32)
    third = send(theirs, other_both).astype(F32)
    return ((own.astype(F32) + beside) + (across + third)).reshape(4, 24, 1664)


def place_on_z():
    return (lax.axis_index("seq") >> 3) & 3


def scatter_over_z(mine):
    z = place_on_z()
    total = pick(mine, z, 0)
    for k in (1, 2, 3):
        part = pick(mine, z ^ k, 0).astype(BF16)
        total = total + send(part, flip(8 * k)).astype(F32)
    return total


def add_flips(own, a, b):
    first, second, third = (send(own, flip(m)).astype(F32) for m in (a, b, a ^ b))
    return (own.astype(F32) + first) + (second + third)


def place_kernel(z, *refs):
    out = refs[-1]
    for k in range(4):
        out[pl.ds(z[0] ^ k, 1)] = refs[k][...][None]


def gather_over_z(total, *after):
    found = [total] + [send(total, flip(8 * k)) for k in (1, 2, 3)]
    return pl.pallas_call(
        place_kernel,
        in_specs=[pl.BlockSpec(memory_space=pltpu.SMEM)]
        + [pl.BlockSpec(memory_space=pltpu.VMEM)] * 4
        + [pl.BlockSpec(memory_space=pl.ANY)] * len(after),
        out_shape=jax.ShapeDtypeStruct((4, 24, 1664), BF16),
        compiler_params=params(),
    )(place_on_z().reshape(1), *found, *after)


def result_kernel(core, own, across, taps, mix, bias):
    for source, base in ((own, 96 * core[0]), (across, 96 * (1 - core[0]))):
        for j in range(4):
            place = pl.ds(pl.multiple_of(base + 24 * j, 8), 24)
            block = source[j].astype(F32)
            for k in range(3):
                taps[k, place, :] = block[:, 384 * k : 384 * (k + 1)]
            mix[place, :] = block[:, 1152:1536]
            bias[place, :] = block[:, 1536:1664]


def results(gathered):
    core = (lax.axis_index("seq") & 1).reshape(1)
    vmem = pl.BlockSpec(memory_space=pltpu.VMEM)
    taps, mix, bias = pl.pallas_call(
        result_kernel,
        in_specs=[pl.BlockSpec(memory_space=pltpu.SMEM), vmem, vmem],
        out_specs=[vmem] * 3,
        out_shape=[
            jax.ShapeDtypeStruct((3, 192, 384), F32),
            jax.ShapeDtypeStruct((192, 384), F32),
            jax.ShapeDtypeStruct((192, 128), F32),
        ],
        compiler_params=params(),
    )(core, gathered, send(gathered, other_core))
    return taps, bias[:, 0], mix


def edges(chip, core):
    first, final = (chip == 0).astype(jnp.int32), (chip == 31).astype(jnp.int32)
    one, zero = jnp.int32(1), jnp.int32(0)
    behind, ahead = jnp.stack([zero, 1 - first]), jnp.stack([final, one])
    return jnp.concatenate(
        [
            jnp.where(core == 0, behind, ahead),
            jnp.stack([1 - first, one]),
            jnp.where(core == 0, ahead, behind),
            jnp.stack([one, 1 - final, core]),
        ]
    )


def per_device(inputs, convolution_weight, conv_bias, mix_weight, cotangent):
    factor = 1.0 / math.sqrt(inputs.shape[0] * inputs.shape[2] * lax.axis_size("seq"))
    edge = edges((lax.axis_index("seq") >> 1) & 31, lax.axis_index("seq") & 1)
    field = (2, 2, 192, SIZE)
    column = jnp.stack([lax.axis_index("ch"), lax.axis_index("seq") >> 6]).astype(jnp.int32)
    here = [gather_column(inputs, column, k) for k in range(CHUNKS)]
    weights = pack_weights(convolution_weight, mix_weight, conv_bias, here[-1])
    weights = gather_weights(weights, lax.axis_index("ch"), lax.axis_index("seq") & 1)
    cot = [exchange(pack(cotangent, k, weights)).reshape(field) for k in range(CHUNKS)]
    sides = [(send(a, chips_on(1)), send(a, chips_on(-1))) for a in here]
    sums, acts, grads, grad_sides = (), [], [], []
    for k in range(CHUNKS):
        act, grad, *sums = middle(edge, sides[k][0], here[k], sides[k][1], cot[k], weights)
        acts.append(act)
        grads.append(grad)
        grad_sides.append((send(grad, chips_on(1)), send(grad, chips_on(-1))))

    def flat(piece):
        return piece.reshape(4, 192, SIZE)

    own, theirs = add_cores(lax.axis_index("ch"), sums[0], send(sums[1], other_core))
    mine = sum_in_column(own, theirs)
    out, taps = mixed(edge, here[0], acts[0], weights, mine)
    outs = [exchange(flat(out))]
    total = scatter_over_z(mine).astype(BF16)
    input_grads = [
        back(edge, grad_sides[k][0], grads[k], grad_sides[k][1], cot[k], taps, *outs)
        for k in range(CHUNKS)
    ]
    input_parts = [exchange(flat(p)) for p, _ in input_grads]
    outputs, _ = unpack(outs)
    input_grad, unpacked = unpack(input_parts)
    total = total.astype(F32) + send(total, flip(32)).astype(F32)
    total = add_flips(rounded(total, *[token for _, token in input_grads]), 2, 4)
    gathered = gather_over_z((total * factor).astype(BF16), unpacked)
    weight_grad, bias_grad, mix_grad = results(gathered)
    return outputs, input_grad, weight_grad, bias_grad, mix_grad


def solution(mesh):
    in_specs = (
        P(None, "ch", "seq"),
        P(None, "ch", None),
        P("ch"),
        P("ch", None),
        P(None, "ch", "seq"),
    )
    out_specs = (
        P(None, "ch", "seq"),
        P(None, "ch", "seq"),
        P(None, "ch", None),
        P("ch"),
        P("ch", None),
    )
    return jax.shard_map(
        per_device, mesh=mesh, in_specs=in_specs, out_specs=out_specs, check_vma=False
    )
```
